256 devices in a mesh: grp: 4 (over z_hi), dev: 64 (over z_lo, y, x, core).
Axes of the slice: x: 4, y: 4, z: 8 (z_hi: 4, z_lo: 2; z = z_hi * 2 + z_lo), core: 2. Of those that a mesh axis runs over, the one named last changes fastest.
Arguments:
- series: float32 [2, 33554432], P(None, ('grp', 'dev')), may hold values from -6 to 6
Outputs:
- spectrum: float32 [2, 33554432], P(None, ('grp', 'dev'))
The draws below stay inside these ranges and needn't reach their ends.
All inputs are finite; a program needn't handle non-finite values.
Results may differ from the reference program's by a relative error of at most 0.00007.
Values sent between devices are 32-bit elements; how exact they have to be, the bound alone decides.
A program may use at most 128 MiB of HBM per device.

```python
import math
import jax
import jax.numpy as jnp

POINTS = 33554432


def steps_of(rng, dims, shards, smallest, largest):
    loudness, own = 1.0, jax.random.fold_in(rng, 6)
    for axis_at, blocks in shards:
        heights = jnp.exp(jax.random.uniform(jax.random.fold_in(own, axis_at), (blocks,), jnp.float32, smallest / len(shards), largest / len(shards)))
        loudness = loudness * jnp.repeat(heights, dims[axis_at] // blocks).reshape([-1 if axis == axis_at else 1 for axis in range(len(dims))])
    return loudness


def bell_draw(rng, extent, scale, reach, shards=(), dtype=jnp.bfloat16):
    level = steps_of(rng, extent, shards, -0.22, 0.18) if shards else 1.0
    array = jax.random.normal(rng, extent, jnp.float32) * scale * level
    return jnp.minimum(jnp.maximum(array, -reach), reach).astype(dtype)


def setup_inputs(seed: int = 0) -> dict:
    splits = jax.random.split(jax.random.key(seed), 2)
    return {
        "series": bell_draw(splits[0], (2, POINTS), 1.0, 6.0, ((1, 256),), jnp.float32),
    }


def reference(series):
    scaled = series * (1.0 / math.sqrt(POINTS))
    signal = scaled[0] + 1j * scaled[1]
    result = jnp.fft.fft(signal)
    return jnp.stack([jnp.real(result), jnp.imag(result)])
```

```python
import math

import jax
import jax.numpy as jnp
import ml_dtypes
import numpy as np
from jax import lax
from jax.experimental import pallas as pl
from jax.experimental.pallas import tpu as pltpu
from jax.sharding import PartitionSpec as P

MESH = pl.DeviceIdType.MESH
BITS = 25
LANES = 128
PEERS = 256
CHUNKS = 4
ROWS = 512


def split(table):
    high = table.astype(ml_dtypes.bfloat16)
    low = (table - high.astype(np.float64)).astype(ml_dtypes.bfloat16)
    return np.stack([high, low])


def table_256():
    at = np.arange(256)
    angle = 2.0 * np.pi * ((at[:, None] * at[None, :]) % 256) / 256
    cosine, sine = np.cos(angle), np.sin(angle)
    full = np.zeros((2, 256, 256, 2))
    full[0, :, :, 0], full[0, :, :, 1] = cosine, sine
    full[1, :, :, 0], full[1, :, :, 1] = -sine, cosine
    return split(full.reshape(512, 512))


def table_512():
    at = np.arange(512)
    angle = 2.0 * np.pi * ((at[:, None] * at[None, :]) % 512) / 512
    cosine, sine = np.cos(angle), np.sin(angle)
    full = np.zeros((256, 2, 2, 2, 512))
    cosine, sine = cosine.reshape(256, 2, 512), sine.reshape(256, 2, 512)
    full[:, :, 0, 0], full[:, :, 0, 1] = cosine, sine
    full[:, :, 1, 0], full[:, :, 1, 1] = -sine, cosine
    full = full.transpose(1, 0, 2, 3, 4).reshape(2, 512, 1024)
    return split(full)


def turn(steps):
    quarter = (steps + (1 << (BITS - 3))) >> (BITS - 2)
    rest = steps - (quarter << (BITS - 2))
    x = rest.astype(jnp.float32) * (2.0 * math.pi / (1 << BITS))
    y = x * x
    sine = x * (1.0 + y * (-1.0 / 6 + y * (1.0 / 120 + y * (-1.0 / 5040 + y * (1.0 / 362880)))))
    cosine = 1.0 + y * (-0.5 + y * (1.0 / 24 + y * (-1.0 / 720 + y * (1.0 / 40320))))
    odd = (quarter & 1) != 0
    c, s = jnp.where(odd, sine, cosine), jnp.where(odd, cosine, sine)
    c = jnp.where(((quarter + 1) & 2) != 0, -c, c)
    s = jnp.where((quarter & 2) != 0, -s, s)
    return c, s


def shifted(me, i):
    z, y, x, c = me >> 5, (me >> 3) & 3, (me >> 1) & 3, me & 1
    z = (z + (i & 7)) & 7
    c = c ^ ((i >> 3) & 1)
    x = (x + ((i >> 4) & 3)) & 3
    y = (y + ((i >> 6) & 3)) & 3
    return z * 32 + y * 8 + x * 2 + c


def address(device):
    return (device >> 6, device & 63)


def halves(values):
    high = values.astype(jnp.bfloat16)
    return high, (values - high.astype(jnp.float32)).astype(jnp.bfloat16)


def dot(a, b):
    return jnp.dot(a, b, preferred_element_type=jnp.float32)


def dot_t(a, b):
    return lax.dot_general(a, b, (((1,), (1,)), ((), ())), preferred_element_type=jnp.float32)


def kernel(
    x_ref, a_hbm, b_hbm, o_ref,
    r1, s2, r2, s3, r3, out, zb, a, b, t1, t2,
    load_sem, out_sem, ready, self_sem, send_sem, recv_sem,
):
    me = lax.axis_index("grp") * 64 + lax.axis_index("dev")

    barrier = pltpu.get_barrier_semaphore()

    def greet_column(i, carry):
        pl.semaphore_signal(barrier, inc=1, device_id=address(shifted(me, i + 1)), device_id_type=MESH)
        return carry

    def greet_plane(i, carry):
        pl.semaphore_signal(barrier, inc=1, device_id=address(shifted(me, (i + 1) * 8)), device_id_type=MESH)
        return carry

    lax.fori_loop(0, 7, greet_column, 0)
    lax.fori_loop(0, 31, greet_plane, 0)

    load_a = pltpu.make_async_copy(a_hbm, a, load_sem.at[0])
    load_b = pltpu.make_async_copy(b_hbm, b, load_sem.at[1])
    load_a.start()
    load_b.start()

    scale = 1.0 / math.sqrt(1 << BITS)

    def fill(table, row_step, column_start, factor):
        def block(i, carry):
            start = pl.multiple_of(i * 16, 16)
            row = lax.broadcasted_iota(jnp.int32, (16, 512), 0) + start
            column = lax.broadcasted_iota(jnp.int32, (16, 512), 1) + column_start
            c, s = turn(row * column * row_step)
            if factor is not None:
                c, s = c * factor, s * factor
            table[0, pl.ds(start, 16), :] = c
            table[1, pl.ds(start, 16), :] = s
            return carry

        lax.fori_loop(0, 16, block, 0)

    fill(t1, 1, me * 512, scale)

    pl.semaphore_wait(barrier, 38)

    def tell_column(i, carry):
        pl.semaphore_signal(ready, inc=1, device_id=address(shifted(me, i + 1)), device_id_type=MESH)
        return carry

    lax.fori_loop(0, 7, tell_column, 0)
    pl.semaphore_wait(ready, 7)

    def exchange(phase, chunk, source, first, step, target):
        at = phase * CHUNKS + chunk
        own = target.at[pl.ds(chunk * ROWS + me * 2, 2)]

        def send(i, carry):
            other = shifted(me, i + 1)
            pltpu.make_async_remote_copy(
                src_ref=source.at[pl.ds(first + other * step, 2)],
                dst_ref=own,
                send_sem=send_sem.at[at],
                recv_sem=recv_sem.at[at],
                device_id=address(other),
                device_id_type=MESH,
            ).start()
            return carry

        lax.fori_loop(0, PEERS - 1, send, 0)
        pltpu.make_async_copy(source.at[pl.ds(first + me * step, 2)], own, self_sem.at[at]).start()

    def arrived(phase, chunk, target):
        at = phase * CHUNKS + chunk
        rest = target.at[pl.ds(chunk * ROWS, ROWS - 2)]
        one = target.at[pl.ds(chunk * ROWS, 2)]
        pltpu.make_async_copy(one, one, self_sem.at[at]).wait()
        pltpu.make_async_copy(rest, rest, recv_sem.at[at]).wait()

    for q in range(CHUNKS):
        exchange(0, q, x_ref, q * 2, 8, r1)

    fill(t2, 256, 0, None)
    load_a.wait()
    load_b.wait()

    def sum_256(values):
        high, low = halves(values)
        total = dot(a[0], high) + dot(a[0], low) + dot(a[1], high)
        return total[:256], total[256:]

    def rotate(real, imag, table, q):
        c = table[0, :, q * LANES : (q + 1) * LANES]
        s = table[1, :, q * LANES : (q + 1) * LANES]
        return real * c + imag * s, imag * c - real * s

    for q in range(CHUNKS):
        arrived(0, q, r1)
        real, imag = sum_256(r1[q * ROWS : (q + 1) * ROWS, :])
        real, imag = rotate(real, imag, t1, q)
        s2[pl.ds(q * ROWS, 256, stride=2), :] = real
        s2[pl.ds(q * ROWS + 1, 256, stride=2), :] = imag
        exchange(1, q, s2, q * ROWS, 2, r2)

    for q in range(CHUNKS):
        arrived(1, q, r2)
        real, imag = sum_256(r2[q * ROWS : (q + 1) * ROWS, :])
        parts = rotate(real, imag, t2, q)
        for part in range(2):
            columns = slice(part * 512 + q * LANES, part * 512 + (q + 1) * LANES)
            high, low = halves(parts[part])
            for side in range(2):
                zb[side, 0:128, columns] = high[side * 128 : (side + 1) * 128]
                zb[side, 128:256, columns] = low[side * 128 : (side + 1) * 128]

    for h in range(CHUNKS):
        odd, side = h // 2, h % 2
        both = dot_t(b[0, odd], zb[side])
        s3[h * ROWS : (h + 1) * ROWS, :] = (
            both[:, :128] + both[:, 128:] + dot_t(b[1, odd], zb[side, 0:128, :])
        )
        exchange(2, h, s3, h * ROWS, 2, r3)

    for h in range(CHUNKS):
        arrived(2, h, r3)
        for part in range(2):
            flipped = r3[pl.ds(h * ROWS + part, 256, stride=2), :].T
            out[pl.ds(h * ROWS + part, 128, stride=4), :] = flipped[:, :128]
            out[pl.ds(h * ROWS + 2 + part, 128, stride=4), :] = flipped[:, 128:]
        rows = pl.ds(h * ROWS, ROWS)
        pltpu.make_async_copy(out.at[rows], o_ref.at[rows], out_sem.at[h]).start()

    for h in range(CHUNKS):
        rows = pl.ds(h * ROWS, ROWS)
        pltpu.make_async_copy(out.at[rows], o_ref.at[rows], out_sem.at[h]).wait()
    for phase, source in enumerate((x_ref, s2, s3)):
        for chunk in range(CHUNKS):
            sent = source.at[pl.ds(0, ROWS - 2)]
            pltpu.make_async_copy(sent, sent, send_sem.at[phase * CHUNKS + chunk]).wait()


def local(series):
    rows = series.reshape(2, 1024, LANES).transpose(1, 0, 2).reshape(2048, LANES)
    big = pltpu.VMEM((2048, LANES), jnp.float32)
    result = pl.pallas_call(
        kernel,
        out_shape=jax.ShapeDtypeStruct((2048, LANES), jnp.float32),
        in_specs=[pl.BlockSpec(memory_space=pl.ANY)] * 3,
        out_specs=pl.BlockSpec(memory_space=pl.ANY),
        scratch_shapes=[
            big, big, big, big, big, big,
            pltpu.VMEM((2, 256, 1024), jnp.bfloat16),
            pltpu.VMEM((2, 512, 512), jnp.bfloat16),
            pltpu.VMEM((2, 2, 512, 1024), jnp.bfloat16),
            pltpu.VMEM((2, 256, 512), jnp.float32),
            pltpu.VMEM((2, 256, 512), jnp.float32),
            pltpu.SemaphoreType.DMA((2,)),
            pltpu.SemaphoreType.DMA((CHUNKS,)),
            pltpu.SemaphoreType.REGULAR,
            pltpu.SemaphoreType.DMA((3 * CHUNKS,)),
            pltpu.SemaphoreType.DMA((3 * CHUNKS,)),
            pltpu.SemaphoreType.DMA((3 * CHUNKS,)),
        ],
        compiler_params=pltpu.CompilerParams(
            collective_id=0, has_side_effects=True, vmem_limit_bytes=56 * 1024 * 1024
        ),
        cost_estimate=pl.CostEstimate(flops=3_000_000_000, bytes_accessed=8_000_000, transcendentals=0),
    )(rows, jnp.asarray(table_256()), jnp.asarray(table_512()))
    return result.reshape(1024, 2, LANES).transpose(1, 0, 2).reshape(2, 131072)


def solution(mesh):
    return jax.shard_map(
        local,
        mesh=mesh,
        in_specs=(P(None, ("grp", "dev")),),
        out_specs=P(None, ("grp", "dev")),
        check_vma=False,
    )
```

```python
import math

import jax
import jax.numpy as jnp
import ml_dtypes
import numpy as np
from jax import lax
from jax.experimental import pallas as pl
from jax.experimental.pallas import tpu as pltpu
from jax.sharding import PartitionSpec as P

MESH = pl.DeviceIdType.MESH
BITS = 25
LANES = 128
PEERS = 256
CHUNKS = 4
ROWS = 512


def split(table):
    high = table.astype(ml_dtypes.bfloat16)
    low = (table - high.astype(np.float64)).astype(ml_dtypes.bfloat16)
    return np.stack([high, low])


def sum_table(index):
    length = index.size
    angle = 2.0 * np.pi * ((np.arange(length)[:, None] * index[None, :]) % length) / length
    cosine, sine = np.cos(angle), np.sin(angle)
    full = np.zeros((2, length, length, 2))
    full[0, :, :, 0], full[0, :, :, 1] = cosine, sine
    full[1, :, :, 0], full[1, :, :, 1] = -sine, cosine
    return full.reshape(2 * length, 2 * length)


def tables():
    device = np.arange(256)
    first = sum_table(np.concatenate([device * 2, device * 2 + 1]))
    first = first.reshape(2, 2, 256, 1024).transpose(1, 0, 2, 3).reshape(1024, 1024)
    second = sum_table(np.arange(512))
    third = sum_table(np.arange(128)).reshape(256, 128, 2).transpose(0, 2, 1).reshape(256, 256)
    return split(first), split(second), split(third)


def turn(steps):
    quarter = (steps + (1 << (BITS - 3))) >> (BITS - 2)
    rest = steps - (quarter << (BITS - 2))
    x = rest.astype(jnp.float32) * (2.0 * math.pi / (1 << BITS))
    y = x * x
    sine = x * (1.0 + y * (-1.0 / 6 + y * (1.0 / 120 + y * (-1.0 / 5040 + y * (1.0 / 362880)))))
    cosine = 1.0 + y * (-0.5 + y * (1.0 / 24 + y * (-1.0 / 720 + y * (1.0 / 40320))))
    odd = (quarter & 1) != 0
    c, s = jnp.where(odd, sine, cosine), jnp.where(odd, cosine, sine)
    c = jnp.where(((quarter + 1) & 2) != 0, -c, c)
    s = jnp.where((quarter & 2) != 0, -s, s)
    return c, s


def shifted(me, i):
    z, y, x, c = me >> 5, (me >> 3) & 3, (me >> 1) & 3, me & 1
    z = (z + (i & 7)) & 7
    c = c ^ ((i >> 3) & 1)
    x = (x + ((i >> 4) & 3)) & 3
    y = (y + ((i >> 6) & 3)) & 3
    return z * 32 + y * 8 + x * 2 + c


def address(device):
    return (device >> 6, device & 63)


def halves(values):
    high = values.astype(jnp.bfloat16)
    return high, (values - high.astype(jnp.float32)).astype(jnp.bfloat16)


def dot(a, b):
    return jnp.dot(a, b, preferred_element_type=jnp.float32)


def dot_t(a, b):
    return lax.dot_general(a, b, (((1,), (1,)), ((), ())), preferred_element_type=jnp.float32)


def kernel(
    x_ref, a_hbm, b_hbm, c_hbm, o_ref,
    xs, r0, r1, s2, r2, s3, r3, out, zb, acc, a, b, c, t1, t2,
    load_sem, out_sem, ready, self_sem, send_sem, recv_sem,
):
    me = lax.axis_index("grp") * 64 + lax.axis_index("dev")
    plane, spot = me >> 5, me & 31

    barrier = pltpu.get_barrier_semaphore()

    def greet(i, carry):
        pl.semaphore_signal(barrier, inc=1, device_id=address(shifted(me, i)), device_id_type=MESH)
        return carry

    lax.fori_loop(1, 8, greet, 0)
    lax.fori_loop(1, 32, lambda i, carry: greet(i * 8, carry), 0)

    loads = [
        pltpu.make_async_copy(x_ref.at[pl.ds((n16 * 2 + q) * ROWS, ROWS)], xs.at[q * 2 + n16], load_sem.at[q * 2 + n16])
        for q in range(2)
        for n16 in range(2)
    ]
    loads += [
        pltpu.make_async_copy(source, target, load_sem.at[4 + i])
        for i, (source, target) in enumerate(((a_hbm, a), (b_hbm, b), (c_hbm, c)))
    ]
    for load in loads:
        load.start()

    def fill(table, width, entry):
        lane = lax.broadcasted_iota(jnp.int32, (16, LANES), 1)

        def block(i, carry):
            start = pl.multiple_of(i * 16, 16)
            row = lax.broadcasted_iota(jnp.int32, (16, LANES), 0) + start
            for q in range(width):
                cosine, sine = turn(entry(row, q, lane))
                table[0, pl.ds(start, 16), q * LANES : (q + 1) * LANES] = cosine
                table[1, pl.ds(start, 16), q * LANES : (q + 1) * LANES] = sine
            return carry

        lax.fori_loop(0, 32, block, 0)

    fill(t1, 2, lambda row, q, lane: row * (q * 32768 + me * 128 + lane))

    for load in loads[:4]:
        load.wait()
    pl.semaphore_wait(barrier, 38)

    def remote(source, target, device, at):
        pltpu.make_async_remote_copy(
            src_ref=source,
            dst_ref=target,
            send_sem=send_sem.at[at],
            recv_sem=recv_sem.at[at],
            device_id=address(device),
            device_id_type=MESH,
        ).start()

    def finished(like, semaphore):
        pltpu.make_async_copy(like, like, semaphore).wait()

    def along_z():
        own = r0.at[plane]

        def send(i, carry):
            other = shifted(me, i)
            remote(xs.at[2, pl.ds((other >> 5) * 64, 64)], own, other, 0)
            return carry

        lax.fori_loop(1, 8, send, 0)
        pltpu.make_async_copy(xs.at[2, pl.ds(plane * 64, 64)], own, self_sem.at[0]).start()

    def in_plane():
        finished(r0.at[0], self_sem.at[0])
        finished(r0.at[pl.ds(0, 7)], recv_sem.at[0])
        own = r1.at[2, :, pl.ds(spot * 2, 2)]

        def send(i, carry):
            other = shifted(me, i * 8)
            remote(r0.at[:, pl.ds((other & 31) * 2, 2)], own, other, 1)
            return carry

        lax.fori_loop(1, 32, send, 0)
        pltpu.make_async_copy(r0.at[:, pl.ds(spot * 2, 2)], own, self_sem.at[1]).start()

    def in_plane_done():
        finished(xs.at[0, pl.ds(0, 16)], self_sem.at[1])
        finished(xs.at[0, pl.ds(0, ROWS - 16)], recv_sem.at[1])

    def exchange(at, source, own):
        def send(i, carry):
            other = shifted(me, i)
            remote(source(other), own, other, at)
            return carry

        lax.fori_loop(1, PEERS, send, 0, unroll=5)
        pltpu.make_async_copy(source(me), own, self_sem.at[at]).start()

    def arrived(at, rows, target):
        finished(xs.at[0, pl.ds(0, rows)], self_sem.at[at])
        finished(target, recv_sem.at[at])

    def product(table, rows, columns, values):
        high, low = halves(values)
        return dot(table[0, rows, columns], high) + dot(table[0, rows, columns], low) + dot(table[1, rows, columns], high)

    everything, half = slice(0, 1024), (slice(0, 512), slice(512, 1024))

    def rotate(real, imag, cosine, sine):
        return real * cosine + imag * sine, imag * cosine - real * sine

    def first_sum(k8, q, total):
        rows, lanes = slice(k8 * 256, (k8 + 1) * 256), slice(q * LANES, (q + 1) * LANES)
        real, imag = rotate(total[:256], total[256:], t1[0, rows, lanes], t1[1, rows, lanes])
        s2[k8 * 2 + q, pl.ds(0, 256, stride=2), :] = real
        s2[k8 * 2 + q, pl.ds(1, 256, stride=2), :] = imag

    def first_whole(k8, q):
        first_sum(k8, q, product(a, half[k8], everything, r1[q * 2 : q * 2 + 2].reshape(1024, LANES)))

    def second_sum(total):
        for part, values in enumerate(rotate(total[:512], total[512:], t2[0], t2[1])):
            lanes = slice(part * LANES, (part + 1) * LANES)
            zb[0, :, lanes], zb[1, :, lanes] = halves(values)

    def third_sum(k8, k16):
        for k17 in range(2):
            rows = slice((k17 * 2 + k16) * LANES, (k17 * 2 + k16 + 1) * LANES)
            total = dot_t(c[0], zb[0, rows]) + dot_t(c[0], zb[1, rows]) + dot_t(c[1], zb[0, rows])
            for part in range(2):
                s3[k8 * 2 + k16, pl.ds(k17 * 2 + part, 128, stride=4), :] = total[part * 128 : (part + 1) * 128]

    def tell(i, carry):
        pl.semaphore_signal(ready, inc=1, device_id=address(shifted(me, i)), device_id_type=MESH)
        return carry

    def pair(buffer, chunk, count):
        def of(device):
            return buffer.at[pl.ds(chunk, count), pl.ds(device * 2, 2)]

        return of

    most = xs.at[0, pl.ds(0, ROWS - 2)]
    two = xs.at[pl.ds(0, 2), pl.ds(0, ROWS - 2)]

    lax.fori_loop(1, 8, tell, 0)
    along_z()
    pl.semaphore_wait(ready, 7)
    exchange(2, pair(xs, 0, 2), r1.at[pl.ds(0, 2), plane, pl.ds(spot * 2, 2)])
    in_plane()
    exchange(3, pair(xs, 3, 1), r1.at[pl.ds(3, 1), plane, pl.ds(spot * 2, 2)])
    fill(t2, 1, lambda row, q, lane: row * lane * 512)
    for load in loads[4:]:
        load.wait()
    arrived(2, 4, two)
    first_whole(0, 0)
    exchange(4, pair(s2, 0, 1), pair(r2, 0, 1)(me))
    in_plane_done()
    acc[0:512, :] = product(a, half[0], half[0], r1[2].reshape(512, LANES))
    arrived(3, 2, most)
    first_sum(0, 1, acc[0:512, :] + product(a, half[0], half[1], r1[3].reshape(512, LANES)))
    exchange(5, pair(s2, 1, 1), pair(r2, 1, 1)(me))
    first_whole(1, 0)
    first_whole(1, 1)
    exchange(6, pair(s2, 2, 2), pair(r2, 2, 2)(me))
    arrived(4, 2, most)
    acc[...] = product(b, everything, half[0], r2[0])
    arrived(5, 2, most)
    second_sum(acc[...] + product(b, everything, half[1], r2[1]))
    third_sum(0, 0)
    exchange(7, pair(s3, 0, 1), pair(r3, 0, 1)(me))
    third_sum(0, 1)
    exchange(8, pair(s3, 1, 1), pair(r3, 1, 1)(me))
    arrived(6, 4, two)
    second_sum(product(b, everything, everything, r2[2:4].reshape(1024, LANES)))
    third_sum(1, 0)
    exchange(9, pair(s3, 2, 1), pair(r3, 2, 1)(me))
    third_sum(1, 1)
    exchange(10, pair(s3, 3, 1), pair(r3, 3, 1)(me))

    def store(k16):
        rows = pl.ds(k16 * 1024, 1024)
        return pltpu.make_async_copy(out.at[rows], o_ref.at[rows], out_sem.at[k16])

    for k8 in range(2):
        for k16 in range(2):
            chunk = k8 * 2 + k16
            arrived(7 + chunk, 2, most)
            for part in range(2):
                flipped = r3[chunk, pl.ds(part, 256, stride=2), :].T
                first = k16 * 1024 + k8 * 4 + part
                out[pl.ds(first, 128, stride=8), :] = flipped[:, :128]
                out[pl.ds(first + 2, 128, stride=8), :] = flipped[:, 128:]
            if k8 == 1:
                store(k16).start()

    for k16 in range(2):
        store(k16).wait()
    finished(xs.at[0, pl.ds(0, ROWS - 64)], send_sem.at[0])
    finished(xs.at[0, pl.ds(0, ROWS - 16)], send_sem.at[1])
    for at in range(2, 11):
        finished(two if at in (2, 6) else most, send_sem.at[at])


def local(series):
    rows = series.reshape(2, 1024, LANES).transpose(1, 0, 2).reshape(2048, LANES)
    chunks = pltpu.VMEM((CHUNKS, ROWS, LANES), jnp.float32)
    result = pl.pallas_call(
        kernel,
        out_shape=jax.ShapeDtypeStruct((2048, LANES), jnp.float32),
        in_specs=[pl.BlockSpec(memory_space=pl.ANY)] * 4,
        out_specs=pl.BlockSpec(memory_space=pl.ANY),
        scratch_shapes=[
            chunks,
            pltpu.VMEM((8, 64, LANES), jnp.float32),
            pltpu.VMEM((4, 8, 64, LANES), jnp.float32),
            chunks, chunks, chunks, chunks,
            pltpu.VMEM((2048, LANES), jnp.float32),
            pltpu.VMEM((2, 512, 256), jnp.bfloat16),
            pltpu.VMEM((1024, LANES), jnp.float32),
            pltpu.VMEM((2, 1024, 1024), jnp.bfloat16),
            pltpu.VMEM((2, 1024, 1024), jnp.bfloat16),
            pltpu.VMEM((2, 256, 256), jnp.bfloat16),
            pltpu.VMEM((2, 512, 256), jnp.float32),
            pltpu.VMEM((2, 512, 128), jnp.float32),
            pltpu.SemaphoreType.DMA((7,)),
            pltpu.SemaphoreType.DMA((2,)),
            pltpu.SemaphoreType.REGULAR,
            pltpu.SemaphoreType.DMA((11,)),
            pltpu.SemaphoreType.DMA((11,)),
            pltpu.SemaphoreType.DMA((11,)),
        ],
        compiler_params=pltpu.CompilerParams(
            collective_id=0, has_side_effects=True, vmem_limit_bytes=56 * 1024 * 1024
        ),
        cost_estimate=pl.CostEstimate(flops=3_000_000_000, bytes_accessed=8_000_000, transcendentals=0),
    )(rows, *(jnp.asarray(table) for table in tables()))
    result = result * (1.0 / math.sqrt(1 << BITS))
    return result.reshape(1024, 2, LANES).transpose(1, 0, 2).reshape(2, 131072)


def solution(mesh):
    return jax.shard_map(
        local,
        mesh=mesh,
        in_specs=(P(None, ("grp", "dev")),),
        out_specs=P(None, ("grp", "dev")),
        check_vma=False,
    )
```

```python
import math

import jax
import jax.numpy as jnp
import ml_dtypes
import numpy as np
from jax import lax
from jax.experimental import pallas as pl
from jax.experimental.pallas import tpu as pltpu
from jax.sharding import PartitionSpec as P

MESH = pl.DeviceIdType.MESH
BITS = 25
LANES = 128
PEERS = 256
CHUNKS = 4
ROWS = 512


def split(table):
    high = table.astype(ml_dtypes.bfloat16)
    low = (table - high.astype(np.float64)).astype(ml_dtypes.bfloat16)
    return np.stack([high, low])


def sum_table(index):
    length = index.size
    angle = 2.0 * np.pi * ((np.arange(length)[:, None] * index[None, :]) % length) / length
    cosine, sine = np.cos(angle), np.sin(angle)
    full = np.zeros((2, length, length, 2))
    full[0, :, :, 0], full[0, :, :, 1] = cosine, sine
    full[1, :, :, 0], full[1, :, :, 1] = -sine, cosine
    return full.reshape(2 * length, 2 * length)


def tables():
    device = np.arange(256)
    first = sum_table(np.concatenate([device * 2, device * 2 + 1]))
    first = first.reshape(2, 2, 256, 1024).transpose(1, 0, 2, 3).reshape(1024, 1024)
    second = sum_table(np.arange(512))
    third = sum_table(np.arange(128)).reshape(256, 128, 2).transpose(0, 2, 1).reshape(256, 256)
    return split(np.concatenate([first, second, np.pad(third, ((0, 0), (0, 768)))]))


def turn(steps):
    quarter = (steps + (1 << (BITS - 3))) >> (BITS - 2)
    rest = steps - (quarter << (BITS - 2))
    x = rest.astype(jnp.float32) * (2.0 * math.pi / (1 << BITS))
    y = x * x
    sine = x * (1.0 + y * (-1.0 / 6 + y * (1.0 / 120 + y * (-1.0 / 5040 + y * (1.0 / 362880)))))
    cosine = 1.0 + y * (-0.5 + y * (1.0 / 24 + y * (-1.0 / 720 + y * (1.0 / 40320))))
    odd = (quarter & 1) != 0
    c, s = jnp.where(odd, sine, cosine), jnp.where(odd, cosine, sine)
    c = jnp.where(((quarter + 1) & 2) != 0, -c, c)
    s = jnp.where((quarter & 2) != 0, -s, s)
    return c, s


def shifted(me, i):
    z, y, x, c = me >> 5, (me >> 3) & 3, (me >> 1) & 3, me & 1
    z = (z + (i & 7)) & 7
    c = c ^ ((i >> 3) & 1)
    x = (x + ((i >> 4) & 3)) & 3
    y = (y + ((i >> 6) & 3)) & 3
    return z * 32 + y * 8 + x * 2 + c


def address(device):
    return (device >> 6, device & 63)


def halves(values):
    high = values.astype(jnp.bfloat16)
    return high, (values - high.astype(jnp.float32)).astype(jnp.bfloat16)


def dot(a, b):
    return jnp.dot(a, b, preferred_element_type=jnp.float32)


def dot_t(a, b):
    return lax.dot_general(a, b, (((1,), (1,)), ((), ())), preferred_element_type=jnp.float32)


def kernel(
    x_ref, tables_ref, o_ref,
    xs, r0, r1, s2, r2, s3, r3, out, zb, acc, a, b, c, t1, t2,
    load_sem, out_sem, ready, self_sem, send_sem, recv_sem,
):
    me = lax.axis_index("grp") * 64 + lax.axis_index("dev")
    plane, spot = me >> 5, me & 31

    barrier = pltpu.get_barrier_semaphore()

    def greet(i, carry):
        pl.semaphore_signal(barrier, inc=1, device_id=address(shifted(me, i)), device_id_type=MESH)
        return carry

    lax.fori_loop(1, 8, greet, 0)
    lax.fori_loop(1, 32, lambda i, carry: greet(i * 8, carry), 0)

    loads = [
        pltpu.make_async_copy(x_ref.at[pl.ds((n16 * 2 + q) * ROWS, ROWS)], xs.at[q * 2 + n16], load_sem.at[q * 2 + n16])
        for q in range(2)
        for n16 in range(2)
    ]
    loads += [
        pltpu.make_async_copy(source, target, load_sem.at[4 + i])
        for i, (source, target) in enumerate(
            (
                (tables_ref.at[:, pl.ds(0, 1024)], a),
                (tables_ref.at[:, pl.ds(1024, 1024)], b),
                (tables_ref.at[:, pl.ds(2048, 256), pl.ds(0, 256)], c),
            )
        )
    ]
    for load in loads:
        load.start()

    def fill(table, width, entry):
        lane = lax.broadcasted_iota(jnp.int32, (16, LANES), 1)

        def block(i, carry):
            start = pl.multiple_of(i * 16, 16)
            row = lax.broadcasted_iota(jnp.int32, (16, LANES), 0) + start
            for q in range(width):
                cosine, sine = turn(entry(row, q, lane))
                table[0, pl.ds(start, 16), q * LANES : (q + 1) * LANES] = cosine
                table[1, pl.ds(start, 16), q * LANES : (q + 1) * LANES] = sine
            return carry

        lax.fori_loop(0, 32, block, 0)

    fill(t1, 2, lambda row, q, lane: row * (q * 32768 + me * 128 + lane))

    for load in loads[:4]:
        load.wait()
    pl.semaphore_wait(barrier, 38)

    def remote(source, target, device, at):
        pltpu.make_async_remote_copy(
            src_ref=source,
            dst_ref=target,
            send_sem=send_sem.at[at],
            recv_sem=recv_sem.at[at],
            device_id=address(device),
            device_id_type=MESH,
        ).start()

    def finished(like, semaphore):
        pltpu.make_async_copy(like, like, semaphore).wait()

    def along_z():
        own = r0.at[plane]

        def send(i, carry):
            other = shifted(me, i)
            remote(xs.at[2, pl.ds((other >> 5) * 64, 64)], own, other, 0)
            return carry

        lax.fori_loop(1, 8, send, 0)
        pltpu.make_async_copy(xs.at[2, pl.ds(plane * 64, 64)], own, self_sem.at[0]).start()

    def in_plane():
        finished(r0.at[0], self_sem.at[0])
        finished(r0.at[pl.ds(0, 7)], recv_sem.at[0])
        own = r1.at[2, :, pl.ds(spot * 2, 2)]

        def send(i, carry):
            other = shifted(me, i * 8)
            remote(r0.at[:, pl.ds((other & 31) * 2, 2)], own, other, 1)
            return carry

        lax.fori_loop(1, 32, send, 0)
        pltpu.make_async_copy(r0.at[:, pl.ds(spot * 2, 2)], own, self_sem.at[1]).start()

    def in_plane_done():
        finished(xs.at[0, pl.ds(0, 16)], self_sem.at[1])
        finished(xs.at[0, pl.ds(0, ROWS - 16)], recv_sem.at[1])

    def exchange(at, source, own):
        def send(i, carry):
            other = shifted(me, i)
            remote(source(other), own, other, at)
            return carry

        lax.fori_loop(1, PEERS, send, 0, unroll=5)
        pltpu.make_async_copy(source(me), own, self_sem.at[at]).start()

    def arrived(at, rows, target):
        finished(xs.at[0, pl.ds(0, rows)], self_sem.at[at])
        finished(target, recv_sem.at[at])

    def product(table, rows, columns, values):
        high, low = halves(values)
        return dot(table[0, rows, columns], high) + dot(table[0, rows, columns], low) + dot(table[1, rows, columns], high)

    everything, half = slice(0, 1024), (slice(0, 512), slice(512, 1024))

    def rotate(real, imag, cosine, sine):
        return real * cosine + imag * sine, imag * cosine - real * sine

    def first_sum(k8, q, total):
        rows, lanes = slice(k8 * 256, (k8 + 1) * 256), slice(q * LANES, (q + 1) * LANES)
        real, imag = rotate(total[:256], total[256:], t1[0, rows, lanes], t1[1, rows, lanes])
        s2[k8 * 2 + q, pl.ds(0, 256, stride=2), :] = real
        s2[k8 * 2 + q, pl.ds(1, 256, stride=2), :] = imag

    def first_whole(k8, q):
        first_sum(k8, q, product(a, half[k8], everything, r1[q * 2 : q * 2 + 2].reshape(1024, LANES)))

    def second_sum(total):
        for part, values in enumerate(rotate(total[:512], total[512:], t2[0], t2[1])):
            lanes = slice(part * LANES, (part + 1) * LANES)
            zb[0, :, lanes], zb[1, :, lanes] = halves(values)

    def third_sum(k8, k16):
        for k17 in range(2):
            rows = slice((k17 * 2 + k16) * LANES, (k17 * 2 + k16 + 1) * LANES)
            total = dot_t(c[0], zb[0, rows]) + dot_t(c[0], zb[1, rows]) + dot_t(c[1], zb[0, rows])
            for part in range(2):
                s3[k8 * 2 + k16, pl.ds(k17 * 2 + part, 128, stride=4), :] = total[part * 128 : (part + 1) * 128]

    def tell(i, carry):
        pl.semaphore_signal(ready, inc=1, device_id=address(shifted(me, i)), device_id_type=MESH)
        return carry

    def pair(buffer, chunk, count):
        def of(device):
            return buffer.at[pl.ds(chunk, count), pl.ds(device * 2, 2)]

        return of

    most = xs.at[0, pl.ds(0, ROWS - 2)]
    two = xs.at[pl.ds(0, 2), pl.ds(0, ROWS - 2)]

    lax.fori_loop(1, 8, tell, 0)
    along_z()
    pl.semaphore_wait(ready, 7)
    exchange(2, pair(xs, 0, 2), r1.at[pl.ds(0, 2), plane, pl.ds(spot * 2, 2)])
    in_plane()
    exchange(3, pair(xs, 3, 1), r1.at[pl.ds(3, 1), plane, pl.ds(spot * 2, 2)])
    fill(t2, 1, lambda row, q, lane: row * lane * 512)
    for load in loads[4:]:
        load.wait()
    arrived(2, 4, two)
    first_whole(0, 0)
    exchange(4, pair(s2, 0, 1), pair(r2, 0, 1)(me))
    in_plane_done()
    acc[0:512, :] = product(a, half[0], half[0], r1[2].reshape(512, LANES))
    arrived(3, 2, most)
    first_sum(0, 1, acc[0:512, :] + product(a, half[0], half[1], r1[3].reshape(512, LANES)))
    exchange(5, pair(s2, 1, 1), pair(r2, 1, 1)(me))
    first_whole(1, 0)
    first_whole(1, 1)
    exchange(6, pair(s2, 2, 2), pair(r2, 2, 2)(me))
    arrived(4, 2, most)
    acc[...] = product(b, everything, half[0], r2[0])
    arrived(5, 2, most)
    second_sum(acc[...] + product(b, everything, half[1], r2[1]))
    third_sum(0, 0)
    exchange(7, pair(s3, 0, 1), pair(r3, 0, 1)(me))
    third_sum(0, 1)
    exchange(8, pair(s3, 1, 1), pair(r3, 1, 1)(me))
    arrived(6, 4, two)
    second_sum(product(b, everything, everything, r2[2:4].reshape(1024, LANES)))
    third_sum(1, 0)
    exchange(9, pair(s3, 2, 1), pair(r3, 2, 1)(me))
    third_sum(1, 1)
    exchange(10, pair(s3, 3, 1), pair(r3, 3, 1)(me))

    def store(k16):
        rows = pl.ds(k16 * 1024, 1024)
        return pltpu.make_async_copy(out.at[rows], o_ref.at[rows], out_sem.at[k16])

    for k8 in range(2):
        for k16 in range(2):
            chunk = k8 * 2 + k16
            arrived(7 + chunk, 2, most)
            for part in range(2):
                flipped = r3[chunk, pl.ds(part, 256, stride=2), :].T
                first = k16 * 1024 + k8 * 4 + part
                out[pl.ds(first, 128, stride=8), :] = flipped[:, :128]
                out[pl.ds(first + 2, 128, stride=8), :] = flipped[:, 128:]
            if k8 == 1:
                store(k16).start()

    for k16 in range(2):
        store(k16).wait()
    finished(xs.at[0, pl.ds(0, ROWS - 64)], send_sem.at[0])
    finished(xs.at[0, pl.ds(0, ROWS - 16)], send_sem.at[1])
    for at in range(2, 11):
        finished(two if at in (2, 6) else most, send_sem.at[at])


def local(series):
    rows = series.reshape(2, 1024, LANES).transpose(1, 0, 2).reshape(2048, LANES)
    chunks = pltpu.VMEM((CHUNKS, ROWS, LANES), jnp.float32)
    result = pl.pallas_call(
        kernel,
        out_shape=jax.ShapeDtypeStruct((2048, LANES), jnp.float32),
        in_specs=[pl.BlockSpec(memory_space=pl.ANY)] * 2,
        out_specs=pl.BlockSpec(memory_space=pl.ANY),
        scratch_shapes=[
            chunks,
            pltpu.VMEM((8, 64, LANES), jnp.float32),
            pltpu.VMEM((4, 8, 64, LANES), jnp.float32),
            chunks, chunks, chunks, chunks,
            pltpu.VMEM((2048, LANES), jnp.float32),
            pltpu.VMEM((2, 512, 256), jnp.bfloat16),
            pltpu.VMEM((1024, LANES), jnp.float32),
            pltpu.VMEM((2, 1024, 1024), jnp.bfloat16),
            pltpu.VMEM((2, 1024, 1024), jnp.bfloat16),
            pltpu.VMEM((2, 256, 256), jnp.bfloat16),
            pltpu.VMEM((2, 512, 256), jnp.float32),
            pltpu.VMEM((2, 512, 128), jnp.float32),
            pltpu.SemaphoreType.DMA((7,)),
            pltpu.SemaphoreType.DMA((2,)),
            pltpu.SemaphoreType.REGULAR,
            pltpu.SemaphoreType.DMA((11,)),
            pltpu.SemaphoreType.DMA((11,)),
            pltpu.SemaphoreType.DMA((11,)),
        ],
        compiler_params=pltpu.CompilerParams(
            collective_id=0, has_side_effects=True, vmem_limit_bytes=52 * 1024 * 1024
        ),
        cost_estimate=pl.CostEstimate(flops=3_000_000_000, bytes_accessed=8_000_000, transcendentals=0),
    )(rows, jnp.asarray(tables()))
    result = result * (1.0 / math.sqrt(1 << BITS))
    return result.reshape(1024, 2, LANES).transpose(1, 0, 2).reshape(2, 131072)


def solution(mesh):
    return jax.shard_map(
        local,
        mesh=mesh,
        in_specs=(P(None, ("grp", "dev")),),
        out_specs=P(None, ("grp", "dev")),
        check_vma=False,
    )
```
